32 devices in a mesh: grp: 1, seq: 8 (over z, y), ch: 4 (over x, core).
Axes of the slice: x: 2, y: 2, z: 4, core: 2. Of those that a mesh axis runs over, the one named last changes fastest.
Arguments:
- inputs: bfloat16 [192, 524288], P('ch', ('grp', 'seq')), may hold values from -6 to 6
- cotangent: bfloat16 [192, 524288], P('ch', ('grp', 'seq')), may hold values from -6 to 6
- kernel: bfloat16 [192, 524288], P('ch', 'seq'), may hold values from 0.25 to 1.75
- right_factor: bfloat16 [1024, 1024], P(('seq', 'ch')), may hold values from -0.1875 to 0.1875
- left_factor: bfloat16 [512, 512], P(('seq', 'ch')), may hold values from -0.25 to 0.25
Outputs:
- mixed_out: bfloat16 [192, 524288], P('ch', ('grp', 'seq'))
- grad_inputs: bfloat16 [192, 524288], P('ch', ('grp', 'seq'))
- grad_kernel: bfloat16 [192, 524288], P('ch', ('grp', 'seq'))
- grad_left: float32 [512, 512], P(('grp', 'seq', 'ch'))
The draws below stay inside these ranges and needn't reach their ends.
All inputs are finite; a program needn't handle non-finite values.
Results may differ from the reference program's by a relative error of at most 0.0058.
Values may be sent and summed in bfloat16 or wider, within the bound.
A program may use at most 192 MiB of HBM per device.

```python
import jax
import jax.numpy as jnp

B1 = 512
B2 = 1024
CH = 192
SEQLEN = 524288


def block_levels(key, extent, cuts, smallest, largest):
    factor_of, own = 1.0, jax.random.fold_in(key, 6)
    for position, parts in cuts:
        steps = jnp.exp(jax.random.uniform(jax.random.fold_in(own, position), (parts,), jnp.float32, smallest / len(cuts), largest / len(cuts)))
        factor_of = factor_of * jnp.repeat(steps, extent[position] // parts).reshape([-1 if axis == position else 1 for axis in range(len(extent))])
    return factor_of


def scatter_about(stream_key, dims, scale, most, split=(), dtype=jnp.bfloat16):
    result = scale * jax.random.normal(stream_key, dims, jnp.float32)
    if split:
        result = result * block_levels(stream_key, dims, split, -0.22, 0.18)
    return jnp.clip(result, -most, most).astype(dtype)


def setup_inputs(seed: int = 0, part: int = 0) -> dict:
    splits = jax.random.split(jax.random.key(seed), 6)
    part_splits = jax.random.split(jax.random.fold_in(splits[5], part), 6)
    return {
        "inputs": scatter_about(part_splits[0], (CH, SEQLEN), 1.0, 6.0, ((0, 4), (1, 8))),
        "cotangent": scatter_about(part_splits[1], (CH, SEQLEN), 1.0, 6.0, ((0, 4), (1, 8))),
        "kernel": jnp.clip(0.25 + 1.5 * jax.random.uniform(splits[2], (CH, SEQLEN), jnp.float32) ** block_levels(splits[2], (CH, SEQLEN), ((0, 4), (1, 8)), -0.2, 0.2), 0.25, 1.75).astype(jnp.bfloat16),
        "right_factor": scatter_about(splits[3], (B2, B2), B2 ** -0.5, 0.1875, ((0, 32),)),
        "left_factor": scatter_about(splits[4], (B1, B1), B1 ** -0.5, 0.25, ((0, 32),)),
    }


def reference(inputs, cotangent, kernel, right_factor, left_factor):
    grad_scale = float(CH * B2) ** -0.5
    kern_view = kernel.reshape(CH, B1, B2)
    projected = jnp.dot(inputs.reshape(CH * B1, B2), right_factor, preferred_element_type=jnp.float32).reshape(CH, B1, B2)
    gated_mix = (projected * kern_view.astype(jnp.float32)).astype(jnp.bfloat16)
    left_wide = left_factor.astype(jnp.float32)
    mixed = jnp.einsum("pi,cij->cjp", left_wide, gated_mix.astype(jnp.float32))
    mixed_out = mixed.astype(jnp.bfloat16).reshape(CH, B1 * B2)
    grad_view = cotangent.reshape(CH, B2, B1).astype(jnp.float32)
    grad_mix = jnp.einsum("pi,cjp->cij", left_wide, grad_view).astype(jnp.bfloat16)
    grad_left = jnp.einsum("cjp,cij->pi", grad_view, gated_mix.astype(jnp.float32)) * grad_scale
    grad_kernel = (grad_mix.astype(jnp.float32) * projected).astype(jnp.bfloat16).reshape(CH, B1 * B2)
    grad_proj = (grad_mix.astype(jnp.float32) * kern_view.astype(jnp.float32)).astype(jnp.bfloat16)
    grad_inputs = jnp.dot(grad_proj.reshape(CH * B1, B2), right_factor.T, preferred_element_type=jnp.float32)
    grad_inputs = grad_inputs.astype(jnp.bfloat16).reshape(CH, B1 * B2)
    return (mixed_out, grad_inputs, grad_kernel, grad_left)
```

```python
import functools

import jax
import jax.numpy as jnp
from jax import lax
from jax.experimental import pallas as pl
from jax.experimental.pallas import tpu as pltpu
from jax.sharding import PartitionSpec as P

B1 = 512
B2 = 1024
CH = 192


def plain_shards(inputs, cotangent, kernel, right_factor, left_factor):
    grad_scale = float(CH * B2) ** (-0.5)
    chan_dev = inputs.shape[0]
    seq_count = lax.axis_size("seq")
    loc_rows = B1 // seq_count
    loc_cols = B2 // seq_count
    flat_in = inputs.reshape(chan_dev * loc_rows, B2)
    kern_view = kernel.reshape(chan_dev, loc_rows, B2)
    whole_right = lax.all_gather(right_factor, ("seq", "ch"), axis=0, tiled=True)
    projected = jnp.dot(flat_in, whole_right, preferred_element_type=jnp.float32)
    projected = projected.reshape(chan_dev, loc_rows, B2)
    gated_mix = (projected * kern_view.astype(jnp.float32)).astype(jnp.bfloat16)
    turned = lax.all_to_all(gated_mix, "seq", split_axis=2, concat_axis=1, tiled=True)
    left_whole = lax.all_gather(left_factor, ("seq", "ch"), axis=0, tiled=True)
    mixed = jnp.einsum("pi,cij->cjp", left_whole, turned, preferred_element_type=jnp.float32)
    mixed_out = mixed.astype(jnp.bfloat16).reshape(chan_dev, loc_cols * B1)
    grad_view = cotangent.reshape(chan_dev, loc_cols, B1)
    grad_mix = jnp.einsum(
        "pi,cjp->cij", left_whole, grad_view, preferred_element_type=jnp.float32
    ).astype(jnp.bfloat16)
    left_terms = (
        jnp.einsum("cjp,cij->pi", grad_view, turned, preferred_element_type=jnp.float32)
        * grad_scale
    )
    grad_left = lax.psum_scatter(left_terms, ("seq", "ch"), scatter_dimension=0, tiled=True)
    back_grad = lax.all_to_all(grad_mix, "seq", split_axis=1, concat_axis=2, tiled=True)
    back_wide = back_grad.astype(jnp.float32)
    grad_kernel = (back_wide * projected).astype(jnp.bfloat16).reshape(chan_dev, loc_rows * B2)
    grad_proj = (
        (back_wide * kern_view.astype(jnp.float32))
        .astype(jnp.bfloat16)
        .reshape(chan_dev * loc_rows, B2)
    )
    grad_flat = lax.dot_general(
        grad_proj, whole_right, (((1,), (1,)), ((), ())), preferred_element_type=jnp.float32
    )
    grad_inputs = grad_flat.astype(jnp.bfloat16).reshape(chan_dev, loc_rows * B2)
    return (mixed_out, grad_inputs, grad_kernel, grad_left)


CHUNK = 16
LANES = 128
F32 = jnp.float32
BF16 = jnp.bfloat16
MESH = pl.DeviceIdType.MESH


def mixer_kernel(
    seqs, chs, chunks, x_hbm, g_hbm, k_hbm, right_ref, left_ref,
    mixed_hbm, gin_hbm, gker_hbm, gleft_ref,
    xbuf, kbuf, out_a, out_b, right_all, left_all, left_turned, turn_i, turn_j,
    g_rows, a_send, a_recv, d_send, d_recv, gl_turned, gl_sum, gl_ch, gl_mid, gl_seq,
    io_sem, out_sem, wsend_sem, wrecv_sem, fsend_sem, frecv_sem,
    asend_sem, arecv_sem, dsend_sem, drecv_sem, csend_sem, crecv_sem, ssend_sem, srecv_sem,
):
    me = lax.axis_index("seq")
    mych = lax.axis_index("ch")
    rows = B1 // seqs
    cols = B2 // seqs
    grad_scale = float(CH * B2) ** (-0.5)
    wide = CHUNK * cols

    def seq_peer(t):
        return lax.rem(me + t, seqs)

    def ch_peer(t):
        return lax.rem(mych + t, chs)

    barrier = pltpu.get_barrier_semaphore()

    def hail_seq(t, _):
        pl.semaphore_signal(barrier, inc=1, device_id={"seq": seq_peer(t)}, device_id_type=MESH)
        return 0

    def hail_ch(t, _):
        pl.semaphore_signal(barrier, inc=1, device_id={"ch": ch_peer(t)}, device_id_type=MESH)
        return 0

    lax.fori_loop(1, seqs, hail_seq, 0)
    lax.fori_loop(1, chs, hail_ch, 0)

    def load(src, q, buf, n):
        return pltpu.make_async_copy(src.at[pl.ds(q * CHUNK, CHUNK), :], buf, io_sem.at[n])

    load(g_hbm, 0, xbuf, 0).start()
    left_all[me, mych] = left_ref[...]
    right_all[me, mych] = right_ref[...]
    pl.semaphore_wait(barrier, seqs + chs - 2)

    def left_seq(frm, to):
        return pltpu.make_async_remote_copy(
            left_all.at[frm, mych], left_all.at[frm, mych], wsend_sem.at[0, to],
            wrecv_sem.at[0, frm], device_id={"seq": to}, device_id_type=MESH)

    def right_seq(frm, to):
        return pltpu.make_async_remote_copy(
            right_all.at[frm, mych], right_all.at[frm, mych], wsend_sem.at[1, to],
            wrecv_sem.at[1, frm], device_id={"seq": to}, device_id_type=MESH)

    def left_ch(frm, to):
        return pltpu.make_async_remote_copy(
            left_all.at[:, frm], left_all.at[:, frm], fsend_sem.at[0, to],
            frecv_sem.at[0, frm], device_id={"ch": to}, device_id_type=MESH)

    def right_ch(frm, to):
        return pltpu.make_async_remote_copy(
            right_all.at[:, frm], right_all.at[:, frm], fsend_sem.at[1, to],
            frecv_sem.at[1, frm], device_id={"ch": to}, device_id_type=MESH)

    def each_seq(f):
        def step(t, _):
            f(seq_peer(t))
            return 0
        lax.fori_loop(1, seqs, step, 0)

    def each_ch(f):
        def step(t, _):
            f(ch_peer(t))
            return 0
        lax.fori_loop(1, chs, step, 0)

    each_seq(lambda d: left_seq(me, d).start())
    each_seq(lambda d: right_seq(me, d).start())

    def turn_grad(q):
        load(g_hbm, q, xbuf, 0).wait()

        def spread(j, _):
            for b in range(B1 // LANES):
                turn_j[b, pl.ds(pl.multiple_of(j * CHUNK, CHUNK), CHUNK), :] = xbuf[
                    :, pl.ds(pl.multiple_of(j * B1 + b * LANES, LANES), LANES)].astype(F32)
            return 0

        lax.fori_loop(0, cols, spread, 0, unroll=4)

        def gather(c, _):
            for b in range(B1 // LANES):
                g_rows[q, pl.ds(pl.multiple_of(c * cols, cols), cols), b * LANES:(b + 1) * LANES] = turn_j[
                    b, pl.ds(c, cols, stride=CHUNK), :].astype(BF16)
            return 0

        lax.fori_loop(0, CHUNK, gather, 0)

    def d_copy(q, frm, to):
        return pltpu.make_async_remote_copy(
            d_send.at[q, pl.ds(pl.multiple_of(to * rows, rows), rows), :],
            d_recv.at[q, pl.ds(pl.multiple_of(frm * rows, rows), rows), :],
            dsend_sem.at[q, to], drecv_sem.at[q, frm], device_id={"seq": to}, device_id_type=MESH)

    def a_copy(q, frm, to):
        return pltpu.make_async_remote_copy(
            a_send.at[q, pl.ds(pl.multiple_of(to * rows, rows), rows), :],
            a_recv.at[q, pl.ds(pl.multiple_of(frm * rows, rows), rows), :],
            asend_sem.at[q, to], arecv_sem.at[q, frm], device_id={"seq": to}, device_id_type=MESH)

    def own_copy(send, recv, sem, q):
        mine = pl.ds(pl.multiple_of(me * rows, rows), rows)
        return pltpu.make_async_copy(send.at[q, mine, :], recv.at[q, mine, :], sem.at[q, me])

    def make_d(q):
        def pair(h, _):
            at = pl.multiple_of(h * 2 * cols, 2 * cols)
            d_send[q, :, pl.ds(at, 2 * cols)] = lax.dot_general(
                left_turned[...], g_rows[q, pl.ds(at, 2 * cols), :],
                (((1,), (1,)), ((), ())), preferred_element_type=F32).astype(BF16)
            return 0

        lax.fori_loop(0, CHUNK // 2, pair, 0)

    def project(g):
        lhs = jnp.concatenate(
            [xbuf[:, pl.ds(pl.multiple_of((g * CHUNK + n) * B2, B2), B2)] for n in range(CHUNK)], axis=0)
        return jnp.dot(lhs, right_all[...].reshape(B2, B2), preferred_element_type=F32)

    def gates(g):
        return jnp.concatenate(
            [kbuf[:, pl.ds(pl.multiple_of((g * CHUNK + n) * B2, B2), B2)] for n in range(CHUNK)], axis=0)

    tall = CHUNK * CHUNK

    def make_a(q):
        load(x_hbm, q, xbuf, 0).wait()
        load(k_hbm, q, kbuf, 1).wait()

        def group(g, _):
            gated = project(g) * gates(g).astype(F32)
            for d in range(seqs):
                turn_i[d, pl.ds(pl.multiple_of(g * tall, tall), tall), :] = gated[:, d * cols:(d + 1) * cols]
            return 0

        lax.fori_loop(0, rows // CHUNK, group, 0)

        def gather(c, _):
            at = pl.multiple_of(c * cols, cols)
            for d in range(seqs):
                a_send[q, d * rows:(d + 1) * rows, pl.ds(at, cols)] = turn_i[
                    d, pl.ds(c, rows, stride=CHUNK), :].astype(BF16)
            return 0

        lax.fori_loop(0, CHUNK, gather, 0)

    def send(copy, q, send_buf, recv_buf, sem, earlier):
        own_copy(send_buf, recv_buf, sem, q).start()

        def one(d):
            if earlier is not None:
                earlier[0](earlier[1], me, d).wait_send()
            copy(q, me, d).start()

        each_seq(one)

    def arrived(copy, q, send_buf, recv_buf, sem):
        own_copy(send_buf, recv_buf, sem, q).wait()
        each_seq(lambda d: copy(q, d, me).wait_recv())

    send_d = lambda q, earlier: send(d_copy, q, d_send, d_recv, drecv_sem, earlier)
    send_a = lambda q, earlier: send(a_copy, q, a_send, a_recv, arecv_sem, earlier)

    def store(buf, dst, q, n):
        return pltpu.make_async_copy(buf, dst.at[pl.ds(q * CHUNK, CHUNK), :], out_sem.at[n])

    def finish_a(q):
        arrived(a_copy, q, a_send, a_recv, arecv_sem)

        def pair(h, _):
            at = pl.multiple_of(h * 2 * cols, 2 * cols)
            block = a_recv[q, :, pl.ds(at, 2 * cols)]
            got = jnp.dot(left_all[...].reshape(B1, B1), block, preferred_element_type=F32).T
            for b in range(B1 // LANES):
                lanes = slice(b * LANES, (b + 1) * LANES)
                turn_j[b, pl.ds(2 * h, cols, stride=CHUNK), :] = got[:cols, lanes]
                turn_j[b, pl.ds(2 * h + 1, cols, stride=CHUNK), :] = got[cols:, lanes]
            gl_turned[...] += jnp.dot(
                block, g_rows[q, pl.ds(at, 2 * cols), :], preferred_element_type=F32)
            return 0

        lax.fori_loop(0, CHUNK // 2, pair, 0)

        def spread(j, _):
            for b in range(B1 // LANES):
                out_a[:, pl.ds(pl.multiple_of(j * B1 + b * LANES, LANES), LANES)] = turn_j[
                    b, pl.ds(pl.multiple_of(j * CHUNK, CHUNK), CHUNK), :].astype(BF16)
            return 0

        lax.fori_loop(0, cols, spread, 0, unroll=4)
        store(out_a, mixed_hbm, q, 0).start()
        store(out_a, mixed_hbm, q, 0).wait()

    def finish_d(q):
        load(x_hbm, q, xbuf, 0).start()
        load(k_hbm, q, kbuf, 1).start()
        load(x_hbm, q, xbuf, 0).wait()
        load(k_hbm, q, kbuf, 1).wait()
        arrived(d_copy, q, d_send, d_recv, drecv_sem)

        def gather(c, _):
            at = pl.multiple_of(c * cols, cols)
            for s in range(seqs):
                turn_i[s, pl.ds(c, rows, stride=CHUNK), :] = d_recv[
                    q, s * rows:(s + 1) * rows, pl.ds(at, cols)].astype(F32)
            return 0

        lax.fori_loop(0, CHUNK, gather, 0)

        def group(g, _):
            at = pl.multiple_of(g * tall, tall)
            back = jnp.concatenate([turn_i[s, pl.ds(at, tall), :] for s in range(seqs)], axis=1)
            first = (back * project(g)).astype(BF16)
            for n in range(CHUNK):
                out_a[:, pl.ds(pl.multiple_of((g * CHUNK + n) * B2, B2), B2)] = first[
                    n * CHUNK:(n + 1) * CHUNK]
            inner = (back * gates(g).astype(F32)).astype(BF16)
            second = lax.dot_general(
                inner, right_all[...].reshape(B2, B2), (((1,), (1,)), ((), ())),
                preferred_element_type=F32).astype(BF16)
            for n in range(CHUNK):
                out_b[:, pl.ds(pl.multiple_of((g * CHUNK + n) * B2, B2), B2)] = second[
                    n * CHUNK:(n + 1) * CHUNK]
            return 0

        lax.fori_loop(0, rows // CHUNK, group, 0)
        store(out_a, gker_hbm, q, 0).start()
        store(out_b, gin_hbm, q, 1).start()
        store(out_a, gker_hbm, q, 0).wait()
        store(out_b, gin_hbm, q, 1).wait()

    def load_a(q):
        load(x_hbm, q, xbuf, 0).start()
        load(k_hbm, q, kbuf, 1).start()

    turn_grad(0)
    load_a(0)
    each_seq(lambda d: left_seq(d, me).wait_recv())
    each_ch(lambda c: left_ch(mych, c).start())
    each_ch(lambda c: left_ch(c, mych).wait_recv())
    left_turned[...] = left_all[...].reshape(B1, B1).astype(F32).T.astype(BF16)
    make_d(0)
    each_seq(lambda d: right_seq(d, me).wait_recv())
    each_ch(lambda c: right_ch(mych, c).start())
    send_d(0, None)
    each_ch(lambda c: right_ch(c, mych).wait_recv())
    gl_turned[...] = jnp.zeros_like(gl_turned)

    order = [(d_copy, 0)] + [(a_copy, q) for q in range(chunks)] + [(d_copy, q) for q in range(1, chunks)]
    make_a(0)
    send_a(0, None)
    ready = {("a", 0), ("d", 0)}

    def prepare(kind, q):
        if (kind, q) in ready:
            return
        ready.add((kind, q))
        if kind == "a":
            load_a(q)
            make_a(q)
        else:
            load(g_hbm, q, xbuf, 0).start()
            turn_grad(q)
            make_d(q)

    for n, (copy, q) in enumerate(order):
        kind = "a" if copy is a_copy else "d"
        if n >= 2:
            prepare(kind, q)
            (send_a if kind == "a" else send_d)(q, order[n - 2])
            if n + 1 < len(order):
                after, qa = order[n + 1]
                prepare("a" if after is a_copy else "d", qa)
            was, qw = order[n - 2]
            if was is a_copy:
                finish_a(qw)
            else:
                finish_d(qw)

    def last(copy, q):
        if copy is a_copy:
            finish_a(q)
        else:
            finish_d(q)

    def gl_to_ch(frm, to):
        return pltpu.make_async_remote_copy(
            gl_sum.at[:, to], gl_ch.at[frm], csend_sem.at[to], crecv_sem.at[frm],
            device_id={"ch": to}, device_id_type=MESH)

    def gl_to_seq(frm, to):
        return pltpu.make_async_remote_copy(
            gl_mid.at[to], gl_seq.at[frm], ssend_sem.at[to], srecv_sem.at[frm],
            device_id={"seq": to}, device_id_type=MESH)

    gl_sum[...] = (gl_turned[...].T * grad_scale).reshape(gl_sum.shape)
    each_ch(lambda c: gl_to_ch(mych, c).start())
    gl_ch[mych] = gl_sum[:, mych]
    each_ch(lambda c: gl_to_ch(c, mych).wait_recv())
    total = gl_ch[0]
    for c in range(1, chs):
        total = total + gl_ch[c]
    gl_mid[...] = total
    each_seq(lambda d: gl_to_seq(me, d).start())
    gl_seq[me] = gl_mid[me]

    last(*order[-2])
    each_seq(lambda d: gl_to_seq(d, me).wait_recv())
    whole = gl_seq[0]
    for s in range(1, seqs):
        whole = whole + gl_seq[s]
    gleft_ref[...] = whole
    last(*order[-1])

    for copy, q in order[-2:]:
        each_seq(lambda d: copy(q, me, d).wait_send())
    each_seq(lambda d: left_seq(me, d).wait_send())
    each_seq(lambda d: right_seq(me, d).wait_send())
    each_ch(lambda c: left_ch(mych, c).wait_send())
    each_ch(lambda c: right_ch(mych, c).wait_send())
    each_ch(lambda c: gl_to_ch(mych, c).wait_send())
    each_seq(lambda d: gl_to_seq(me, d).wait_send())


def shards(inputs, cotangent, kernel, right_factor, left_factor):
    seqs, chs = lax.axis_size("seq"), lax.axis_size("ch")
    chan_dev, span = inputs.shape
    rows, cols = B1 // seqs, B2 // seqs
    if chan_dev % CHUNK or cols != LANES or rows % CHUNK or chan_dev < 3 * CHUNK:
        return plain_shards(inputs, cotangent, kernel, right_factor, left_factor)
    chunks = chan_dev // CHUNK
    wide = CHUNK * cols
    any_spec = pl.BlockSpec(memory_space=pl.ANY)
    vmem_spec = pl.BlockSpec(memory_space=pltpu.VMEM)
    dma = pltpu.SemaphoreType.DMA
    big = jax.ShapeDtypeStruct((chan_dev, span), BF16)
    part = B1 // (seqs * chs)
    flops = 2 * chan_dev * B1 * B2 * (3 * B2 + 3 * B1) // seqs
    return pl.pallas_call(
        functools.partial(mixer_kernel, seqs, chs, chunks),
        out_shape=(big, big, big, jax.ShapeDtypeStruct((part, B1), F32)),
        in_specs=[any_spec] * 3 + [vmem_spec] * 2,
        out_specs=(any_spec, any_spec, any_spec, vmem_spec),
        scratch_shapes=[
            pltpu.VMEM((CHUNK, span), BF16),
            pltpu.VMEM((CHUNK, span), BF16),
            pltpu.VMEM((CHUNK, span), BF16),
            pltpu.VMEM((CHUNK, span), BF16),
            pltpu.VMEM((seqs, chs, B2 // (seqs * chs), B2), BF16),
            pltpu.VMEM((seqs, chs, part, B1), BF16),
            pltpu.VMEM((B1, B1), BF16),
            pltpu.VMEM((seqs, CHUNK * rows, cols), F32),
            pltpu.VMEM((B1 // LANES, CHUNK * cols, LANES), F32),
            pltpu.VMEM((chunks, wide, B1), BF16),
            pltpu.VMEM((chunks, B1, wide), BF16),
            pltpu.VMEM((chunks, B1, wide), BF16),
            pltpu.VMEM((chunks, B1, wide), BF16),
            pltpu.VMEM((chunks, B1, wide), BF16),
            pltpu.VMEM((B1, B1), F32),
            pltpu.VMEM((seqs, chs, part, B1), F32),
            pltpu.VMEM((chs, seqs, part, B1), F32),
            pltpu.VMEM((seqs, part, B1), F32),
            pltpu.VMEM((seqs, part, B1), F32),
            dma((2,)), dma((2,)),
            dma((2, seqs)), dma((2, seqs)), dma((2, chs)), dma((2, chs)),
            dma((chunks, seqs)), dma((chunks, seqs)), dma((chunks, seqs)), dma((chunks, seqs)),
            dma((chs,)), dma((chs,)), dma((seqs,)), dma((seqs,)),
        ],
        compiler_params=pltpu.CompilerParams(
            collective_id=0, has_side_effects=True, vmem_limit_bytes=62 * 1024 * 1024),
        cost_estimate=pl.CostEstimate(flops=flops, bytes_accessed=12 * chan_dev * span, transcendentals=0),
        name="monarch_mixer",
    )(inputs, cotangent, kernel, right_factor, left_factor)


def solution(mesh):
    placed = (
        P("ch", ("grp", "seq")),
        P("ch", ("grp", "seq")),
        P("ch", "seq"),
        P(("seq", "ch"), None),
        P(("seq", "ch"), None),
    )
    return jax.shard_map(
        shards,
        mesh=mesh,
        in_specs=placed,
        out_specs=(
            P("ch", ("grp", "seq")),
            P("ch", ("grp", "seq")),
            P("ch", ("grp", "seq")),
            P(("grp", "seq", "ch"), None),
        ),
        check_vma=False,
    )
```

```python
import functools

import jax
import jax.numpy as jnp
from jax import lax
from jax.experimental import pallas as pl
from jax.experimental.pallas import tpu as pltpu
from jax.sharding import PartitionSpec as P

B1 = 512
B2 = 1024
CH = 192


def plain_shards(inputs, cotangent, kernel, right_factor, left_factor):
    grad_scale = float(CH * B2) ** (-0.5)
    chan_dev = inputs.shape[0]
    seq_count = lax.axis_size("seq")
    loc_rows = B1 // seq_count
    loc_cols = B2 // seq_count
    flat_in = inputs.reshape(chan_dev * loc_rows, B2)
    kern_view = kernel.reshape(chan_dev, loc_rows, B2)
    whole_right = lax.all_gather(right_factor, ("seq", "ch"), axis=0, tiled=True)
    projected = jnp.dot(flat_in, whole_right, preferred_element_type=jnp.float32)
    projected = projected.reshape(chan_dev, loc_rows, B2)
    gated_mix = (projected * kern_view.astype(jnp.float32)).astype(jnp.bfloat16)
    turned = lax.all_to_all(gated_mix, "seq", split_axis=2, concat_axis=1, tiled=True)
    left_whole = lax.all_gather(left_factor, ("seq", "ch"), axis=0, tiled=True)
    mixed = jnp.einsum("pi,cij->cjp", left_whole, turned, preferred_element_type=jnp.float32)
    mixed_out = mixed.astype(jnp.bfloat16).reshape(chan_dev, loc_cols * B1)
    grad_view = cotangent.reshape(chan_dev, loc_cols, B1)
    grad_mix = jnp.einsum(
        "pi,cjp->cij", left_whole, grad_view, preferred_element_type=jnp.float32
    ).astype(jnp.bfloat16)
    left_terms = (
        jnp.einsum("cjp,cij->pi", grad_view, turned, preferred_element_type=jnp.float32)
        * grad_scale
    )
    grad_left = lax.psum_scatter(left_terms, ("seq", "ch"), scatter_dimension=0, tiled=True)
    back_grad = lax.all_to_all(grad_mix, "seq", split_axis=1, concat_axis=2, tiled=True)
    back_wide = back_grad.astype(jnp.float32)
    grad_kernel = (back_wide * projected).astype(jnp.bfloat16).reshape(chan_dev, loc_rows * B2)
    grad_proj = (
        (back_wide * kern_view.astype(jnp.float32))
        .astype(jnp.bfloat16)
        .reshape(chan_dev * loc_rows, B2)
    )
    grad_flat = lax.dot_general(
        grad_proj, whole_right, (((1,), (1,)), ((), ())), preferred_element_type=jnp.float32
    )
    grad_inputs = grad_flat.astype(jnp.bfloat16).reshape(chan_dev, loc_rows * B2)
    return (mixed_out, grad_inputs, grad_kernel, grad_left)


CHUNK = 16
LANES = 128
F32 = jnp.float32
BF16 = jnp.bfloat16
MESH = pl.DeviceIdType.MESH


def mixer_kernel(
    seqs, chs, chunks, x_hbm, g_hbm, k_hbm, right_ref, left_ref,
    mixed_hbm, gin_hbm, gker_hbm, gleft_ref,
    xbuf, kbuf, out_a, out_b, right_all, left_all, left_turned, turn_i, turn_j,
    g_rows, a_send, a_recv, d_send, d_recv, gl_turned, gl_sum, gl_ch, gl_mid, gl_side, gl_stand,
    io_sem, out_sem, wsend_sem, wrecv_sem, fsend_sem, frecv_sem,
    asend_sem, arecv_sem, dsend_sem, drecv_sem, csend_sem, crecv_sem, ssend_sem, srecv_sem,
    own_sem, part_sem,
):
    me = lax.axis_index("seq")
    mych = lax.axis_index("ch")
    rows = B1 // seqs
    cols = B2 // seqs
    grad_scale = float(CH * B2) ** (-0.5)
    wide = CHUNK * cols

    def seq_peer(t):
        return lax.rem(me + t, seqs)

    def flip(mask):
        place, bit = 0, 1
        while bit < seqs:
            digit = lax.rem(lax.div(me, bit), 2)
            place = place + bit * (1 - digit if mask & bit else digit)
            bit *= 2
        return place

    def ch_peer(t):
        return lax.rem(mych + t, chs)

    barrier = pltpu.get_barrier_semaphore()

    def hail_seq(t, _):
        pl.semaphore_signal(barrier, inc=1, device_id={"seq": seq_peer(t)}, device_id_type=MESH)
        return 0

    def hail_ch(t, _):
        pl.semaphore_signal(barrier, inc=1, device_id={"ch": ch_peer(t)}, device_id_type=MESH)
        return 0

    lax.fori_loop(1, seqs, hail_seq, 0)
    lax.fori_loop(1, chs, hail_ch, 0)

    def load(src, q, buf, n):
        return pltpu.make_async_copy(src.at[pl.ds(q * CHUNK, CHUNK), :], buf, io_sem.at[n])

    load(g_hbm, 0, xbuf, 0).start()
    left_all[me, mych] = left_ref[...]
    right_all[me, mych] = right_ref[...]
    pl.semaphore_wait(barrier, seqs + chs - 2)

    def left_seq(frm, to):
        return pltpu.make_async_remote_copy(
            left_all.at[frm, mych], left_all.at[frm, mych], wsend_sem.at[0, to],
            wrecv_sem.at[0, frm], device_id={"seq": to}, device_id_type=MESH)

    hops, held, number = [], [0], 0
    bit = seqs // 2
    while bit:
        hops.append([(number + n, mask, bit) for n, mask in enumerate(held)])
        number += len(held)
        held = held + [mask + bit for mask in held]
        bit //= 2

    def right_seq(n, block, to):
        return pltpu.make_async_remote_copy(
            right_all.at[block, mych], right_all.at[block, mych], wsend_sem.at[1, n],
            wrecv_sem.at[1, block], device_id={"seq": to}, device_id_type=MESH)

    def right_hop(h):
        for n, mask, to in hops[h]:
            right_seq(n, flip(mask), flip(to)).start()

    def right_hop_done(h):
        for n, mask, to in hops[h]:
            right_seq(n, flip(mask + to), me).wait_recv()

    def left_ch(frm, to):
        return pltpu.make_async_remote_copy(
            left_all.at[:, frm], left_all.at[:, frm], fsend_sem.at[0, to],
            frecv_sem.at[0, frm], device_id={"ch": to}, device_id_type=MESH)

    def right_ch(frm, to):
        return pltpu.make_async_remote_copy(
            right_all.at[:, frm], right_all.at[:, frm], fsend_sem.at[1, to],
            frecv_sem.at[1, frm], device_id={"ch": to}, device_id_type=MESH)

    def each_seq(f):
        def step(t, _):
            f(seq_peer(t))
            return 0
        lax.fori_loop(1, seqs, step, 0)

    def each_ch(f):
        def step(t, _):
            f(ch_peer(t))
            return 0
        lax.fori_loop(1, chs, step, 0)

    each_seq(lambda d: left_seq(me, d).start())
    right_hop(0)

    def turn_grad(q):
        load(g_hbm, q, xbuf, 0).wait()

        def spread(j, _):
            for b in range(B1 // LANES):
                turn_j[b, pl.ds(pl.multiple_of(j * CHUNK, CHUNK), CHUNK), :] = xbuf[
                    :, pl.ds(pl.multiple_of(j * B1 + b * LANES, LANES), LANES)].astype(F32)
            return 0

        lax.fori_loop(0, cols, spread, 0, unroll=4)

        def gather(c, _):
            for b in range(B1 // LANES):
                g_rows[q, pl.ds(pl.multiple_of(c * cols, cols), cols), b * LANES:(b + 1) * LANES] = turn_j[
                    b, pl.ds(c, cols, stride=CHUNK), :].astype(BF16)
            return 0

        lax.fori_loop(0, CHUNK, gather, 0)

    pieces = rows // CHUNK

    def d_copy(q, g, frm, to):
        return pltpu.make_async_remote_copy(
            d_send.at[q, pl.ds(pl.multiple_of(to * rows + g * CHUNK, CHUNK), CHUNK), :],
            d_recv.at[q, pl.ds(pl.multiple_of(frm * rows + g * CHUNK, CHUNK), CHUNK), :],
            dsend_sem.at[q, g, to], drecv_sem.at[q, g, frm],
            device_id={"seq": to}, device_id_type=MESH)

    def a_copy(q, frm, to):
        return pltpu.make_async_remote_copy(
            a_send.at[q, pl.ds(pl.multiple_of(to * rows, rows), rows), :],
            a_recv.at[q, pl.ds(pl.multiple_of(frm * rows, rows), rows), :],
            asend_sem.at[q, to], arecv_sem.at[q, frm], device_id={"seq": to}, device_id_type=MESH)

    def own_copy(send, recv, q, n):
        mine = pl.ds(pl.multiple_of(me * rows, rows), rows)
        return pltpu.make_async_copy(send.at[q, mine, :], recv.at[q, mine, :], own_sem.at[n, q])

    def make_d(q):
        def pair(h, _):
            at = pl.multiple_of(h * 2 * cols, 2 * cols)
            d_send[q, :, pl.ds(at, 2 * cols)] = lax.dot_general(
                left_turned[...], g_rows[q, pl.ds(at, 2 * cols), :],
                (((1,), (1,)), ((), ())), preferred_element_type=F32).astype(BF16)
            return 0

        lax.fori_loop(0, CHUNK // 2, pair, 0)

    def project(g):
        lhs = jnp.concatenate(
            [xbuf[:, pl.ds(pl.multiple_of((g * CHUNK + n) * B2, B2), B2)] for n in range(CHUNK)], axis=0)
        return jnp.dot(lhs, right_all[...].reshape(B2, B2), preferred_element_type=F32)

    def gates(g):
        return jnp.concatenate(
            [kbuf[:, pl.ds(pl.multiple_of((g * CHUNK + n) * B2, B2), B2)] for n in range(CHUNK)], axis=0)

    tall = CHUNK * CHUNK

    def make_a(q):
        load(x_hbm, q, xbuf, 0).wait()
        load(k_hbm, q, kbuf, 1).wait()

        def group(g, _):
            gated = project(g) * gates(g).astype(F32)
            for d in range(seqs):
                turn_i[d, pl.ds(pl.multiple_of(g * tall, tall), tall), :] = gated[:, d * cols:(d + 1) * cols]
            return 0

        lax.fori_loop(0, rows // CHUNK, group, 0)

        def gather(c, _):
            at = pl.multiple_of(c * cols, cols)
            for d in range(seqs):
                a_send[q, d * rows:(d + 1) * rows, pl.ds(at, cols)] = turn_i[
                    d, pl.ds(c, rows, stride=CHUNK), :].astype(BF16)
            return 0

        lax.fori_loop(0, CHUNK, gather, 0)

    def sent(kind, q, d):
        if kind == "a":
            a_copy(q, me, d).wait_send()
        else:
            for g in range(pieces):
                d_copy(q, g, me, d).wait_send()

    def send_a(q, earlier):
        own_copy(a_send, a_recv, q, 0).start()

        def one(d):
            if earlier is not None:
                sent(*earlier, d)
            a_copy(q, me, d).start()

        each_seq(one)

    def send_d(q, earlier):
        own_copy(d_send, d_recv, q, 1).start()

        def first(d):
            if earlier is not None:
                sent(*earlier, d)
            d_copy(q, 0, me, d).start()

        each_seq(first)

        def later(g, _):
            each_seq(lambda d: d_copy(q, g, me, d).start())
            return 0

        lax.fori_loop(1, pieces, later, 0)

    def store(buf, dst, q, n):
        return pltpu.make_async_copy(buf, dst.at[pl.ds(q * CHUNK, CHUNK), :], out_sem.at[n])

    def finish_a(q):
        own_copy(a_send, a_recv, q, 0).wait()
        each_seq(lambda d: a_copy(q, d, me).wait_recv())

        def pair(h, _):
            at = pl.multiple_of(h * 2 * cols, 2 * cols)
            block = a_recv[q, :, pl.ds(at, 2 * cols)]
            got = jnp.dot(left_all[...].reshape(B1, B1), block, preferred_element_type=F32).T
            for b in range(B1 // LANES):
                lanes = slice(b * LANES, (b + 1) * LANES)
                turn_j[b, pl.ds(2 * h, cols, stride=CHUNK), :] = got[:cols, lanes]
                turn_j[b, pl.ds(2 * h + 1, cols, stride=CHUNK), :] = got[cols:, lanes]
            gl_turned[...] += jnp.dot(
                block, g_rows[q, pl.ds(at, 2 * cols), :], preferred_element_type=F32)
            return 0

        lax.fori_loop(0, CHUNK // 2, pair, 0)

        def spread(j, _):
            for b in range(B1 // LANES):
                out_a[:, pl.ds(pl.multiple_of(j * B1 + b * LANES, LANES), LANES)] = turn_j[
                    b, pl.ds(pl.multiple_of(j * CHUNK, CHUNK), CHUNK), :].astype(BF16)
            return 0

        lax.fori_loop(0, cols, spread, 0, unroll=4)
        store(out_a, mixed_hbm, q, 0).start()
        store(out_a, mixed_hbm, q, 0).wait()

    def finish_d(q):
        load(x_hbm, q, xbuf, 0).start()
        load(k_hbm, q, kbuf, 1).start()
        load(x_hbm, q, xbuf, 0).wait()
        load(k_hbm, q, kbuf, 1).wait()
        own_copy(d_send, d_recv, q, 1).wait()

        def part(buf, dst, g, n):
            span = pl.ds(pl.multiple_of(g * CHUNK * B2, CHUNK * B2), CHUNK * B2)
            return pltpu.make_async_copy(
                buf.at[:, span], dst.at[pl.ds(q * CHUNK, CHUNK), span], part_sem.at[n, g])

        def group(g, _):
            each_seq(lambda d: d_copy(q, g, d, me).wait_recv())
            at = pl.multiple_of(g * tall, tall)

            def gather(c, _):
                lanes = pl.ds(pl.multiple_of(c * cols, cols), cols)
                for s in range(seqs):
                    turn_i[s, pl.ds(at + c, CHUNK, stride=CHUNK), :] = d_recv[
                        q, pl.ds(pl.multiple_of(s * rows + g * CHUNK, CHUNK), CHUNK), lanes].astype(F32)
                return 0

            lax.fori_loop(0, CHUNK, gather, 0, unroll=4)
            back = jnp.concatenate([turn_i[s, pl.ds(at, tall), :] for s in range(seqs)], axis=1)
            inner = (back * gates(g).astype(F32)).astype(BF16)
            second = lax.dot_general(
                inner, right_all[...].reshape(B2, B2), (((1,), (1,)), ((), ())),
                preferred_element_type=F32).astype(BF16)
            for n in range(CHUNK):
                out_b[:, pl.ds(pl.multiple_of((g * CHUNK + n) * B2, B2), B2)] = second[
                    n * CHUNK:(n + 1) * CHUNK]
            part(out_b, gin_hbm, g, 1).start()
            first = (back * project(g)).astype(BF16)
            for n in range(CHUNK):
                out_a[:, pl.ds(pl.multiple_of((g * CHUNK + n) * B2, B2), B2)] = first[
                    n * CHUNK:(n + 1) * CHUNK]
            part(out_a, gker_hbm, g, 0).start()
            return 0

        lax.fori_loop(0, pieces, group, 0)

        def written(g, _):
            part(out_a, gker_hbm, g, 0).wait()
            part(out_b, gin_hbm, g, 1).wait()
            return 0

        lax.fori_loop(0, pieces, written, 0)

    def load_a(q):
        load(x_hbm, q, xbuf, 0).start()
        load(k_hbm, q, kbuf, 1).start()

    turn_grad(0)
    load_a(0)
    each_seq(lambda d: left_seq(d, me).wait_recv())
    each_ch(lambda c: left_ch(mych, c).start())
    each_ch(lambda c: left_ch(c, mych).wait_recv())
    for h in range(1, len(hops) - 1):
        right_hop_done(h - 1)
        right_hop(h)
    left_turned[...] = left_all[...].reshape(B1, B1).astype(F32).T.astype(BF16)
    make_d(0)
    right_hop_done(len(hops) - 2)
    right_hop(len(hops) - 1)
    send_d(0, None)
    right_hop_done(len(hops) - 1)
    each_ch(lambda c: right_ch(mych, c).start())
    each_ch(lambda c: right_ch(c, mych).wait_recv())
    gl_turned[...] = jnp.zeros_like(gl_turned)

    order = [("d", 0)] + [("a", q) for q in range(chunks)] + [("d", q) for q in range(1, chunks)]
    make_a(0)
    send_a(0, None)
    ready = {("a", 0), ("d", 0)}

    def prepare(kind, q):
        if (kind, q) in ready:
            return
        ready.add((kind, q))
        if kind == "a":
            load_a(q)
            make_a(q)
        else:
            load(g_hbm, q, xbuf, 0).start()
            turn_grad(q)
            make_d(q)

    def finish(kind, q):
        if kind == "a":
            finish_a(q)
        else:
            finish_d(q)

    for n, (kind, q) in enumerate(order):
        if n >= 2:
            prepare(kind, q)
            (send_a if kind == "a" else send_d)(q, order[n - 2])
            if n + 1 < len(order):
                prepare(*order[n + 1])
            finish(*order[n - 2])

    def gl_to_ch(frm, to):
        return pltpu.make_async_remote_copy(
            gl_sum.at[:, to], gl_ch.at[frm], csend_sem.at[to], crecv_sem.at[frm],
            device_id={"ch": to}, device_id_type=MESH)

    side = lax.rem(me, 2)
    stand = lax.div(me, 2)

    def gl_to_side(frm, to):
        return pltpu.make_async_remote_copy(
            gl_mid.at[:, to], gl_side, ssend_sem.at[seqs - 1], srecv_sem.at[seqs - 1],
            device_id={"seq": flip(1)}, device_id_type=MESH)

    def gl_to_stand(frm, to):
        return pltpu.make_async_remote_copy(
            gl_side.at[to], gl_stand.at[frm], ssend_sem.at[to], srecv_sem.at[frm],
            device_id={"seq": to * 2 + side}, device_id_type=MESH)

    def each_stand(f):
        def step(t, _):
            f(lax.rem(stand + t, seqs // 2))
            return 0
        lax.fori_loop(1, seqs // 2, step, 0)

    gl_sum[...] = (gl_turned[...].T * grad_scale).reshape(gl_sum.shape)
    each_ch(lambda c: gl_to_ch(mych, c).start())
    gl_ch[mych] = gl_sum[:, mych]
    each_ch(lambda c: gl_to_ch(c, mych).wait_recv())
    total = gl_ch[0]
    for c in range(1, chs):
        total = total + gl_ch[c]
    gl_mid[...] = total.reshape(gl_mid.shape)
    gl_to_side(side, 1 - side).start()
    gl_to_side(1 - side, side).wait_recv()
    gl_side[...] += gl_mid[:, side]
    each_stand(lambda z: gl_to_stand(stand, z).start())
    gl_stand[stand] = gl_side[stand]

    finish(*order[-2])
    each_stand(lambda z: gl_to_stand(z, stand).wait_recv())
    whole = gl_stand[0]
    for z in range(1, seqs // 2):
        whole = whole + gl_stand[z]
    gleft_ref[...] = whole
    finish(*order[-1])

    for kind, q in order[-2:]:
        each_seq(lambda d: sent(kind, q, d))
    each_seq(lambda d: left_seq(me, d).wait_send())
    for hop in hops:
        for n, mask, to in hop:
            right_seq(n, flip(mask), flip(to)).wait_send()
    each_ch(lambda c: left_ch(mych, c).wait_send())
    each_ch(lambda c: right_ch(mych, c).wait_send())
    each_ch(lambda c: gl_to_ch(mych, c).wait_send())
    gl_to_side(side, 1 - side).wait_send()
    each_stand(lambda z: gl_to_stand(stand, z).wait_send())


def shards(inputs, cotangent, kernel, right_factor, left_factor):
    seqs, chs = lax.axis_size("seq"), lax.axis_size("ch")
    chan_dev, span = inputs.shape
    rows, cols = B1 // seqs, B2 // seqs
    if chan_dev % CHUNK or cols != LANES or seqs & (seqs - 1) or seqs < 4 or rows % CHUNK or chan_dev < 3 * CHUNK:
        return plain_shards(inputs, cotangent, kernel, right_factor, left_factor)
    chunks = chan_dev // CHUNK
    wide = CHUNK * cols
    any_spec = pl.BlockSpec(memory_space=pl.ANY)
    vmem_spec = pl.BlockSpec(memory_space=pltpu.VMEM)
    dma = pltpu.SemaphoreType.DMA
    big = jax.ShapeDtypeStruct((chan_dev, span), BF16)
    part = B1 // (seqs * chs)
    flops = 2 * chan_dev * B1 * B2 * (3 * B2 + 3 * B1) // seqs
    return pl.pallas_call(
        functools.partial(mixer_kernel, seqs, chs, chunks),
        out_shape=(big, big, big, jax.ShapeDtypeStruct((part, B1), F32)),
        in_specs=[any_spec] * 3 + [vmem_spec] * 2,
        out_specs=(any_spec, any_spec, any_spec, vmem_spec),
        scratch_shapes=[
            pltpu.VMEM((CHUNK, span), BF16),
            pltpu.VMEM((CHUNK, span), BF16),
            pltpu.VMEM((CHUNK, span), BF16),
            pltpu.VMEM((CHUNK, span), BF16),
            pltpu.VMEM((seqs, chs, B2 // (seqs * chs), B2), BF16),
            pltpu.VMEM((seqs, chs, part, B1), BF16),
            pltpu.VMEM((B1, B1), BF16),
            pltpu.VMEM((seqs, CHUNK * rows, cols), F32),
            pltpu.VMEM((B1 // LANES, CHUNK * cols, LANES), F32),
            pltpu.VMEM((chunks, wide, B1), BF16),
            pltpu.VMEM((chunks, B1, wide), BF16),
            pltpu.VMEM((chunks, B1, wide), BF16),
            pltpu.VMEM((chunks, B1, wide), BF16),
            pltpu.VMEM((chunks, B1, wide), BF16),
            pltpu.VMEM((B1, B1), F32),
            pltpu.VMEM((seqs, chs, part, B1), F32),
            pltpu.VMEM((chs, seqs, part, B1), F32),
            pltpu.VMEM((seqs // 2, 2, part, B1), F32),
            pltpu.VMEM((seqs // 2, part, B1), F32),
            pltpu.VMEM((seqs // 2, part, B1), F32),
            dma((2,)), dma((1,)),
            dma((2, seqs)), dma((2, seqs)), dma((2, chs)), dma((2, chs)),
            dma((chunks, seqs)), dma((chunks, seqs)),
            dma((chunks, rows // CHUNK, seqs)), dma((chunks, rows // CHUNK, seqs)),
            dma((chs,)), dma((chs,)), dma((seqs,)), dma((seqs,)),
            dma((2, chunks)), dma((2, rows // CHUNK)),
        ],
        compiler_params=pltpu.CompilerParams(
            collective_id=0, has_side_effects=True, vmem_limit_bytes=62 * 1024 * 1024),
        cost_estimate=pl.CostEstimate(flops=flops, bytes_accessed=12 * chan_dev * span, transcendentals=0),
        name="monarch_mixer",
    )(inputs, cotangent, kernel, right_factor, left_factor)


def solution(mesh):
    placed = (
        P("ch", ("grp", "seq")),
        P("ch", ("grp", "seq")),
        P("ch", "seq"),
        P(("seq", "ch"), None),
        P(("seq", "ch"), None),
    )
    return jax.shard_map(
        shards,
        mesh=mesh,
        in_specs=placed,
        out_specs=(
            P("ch", ("grp", "seq")),
            P("ch", ("grp", "seq")),
            P("ch", ("grp", "seq")),
            P(("grp", "seq", "ch"), None),
        ),
        check_vma=False,
    )
```

```python
import functools

import jax
import jax.numpy as jnp
from jax import lax
from jax.experimental import pallas as pl
from jax.experimental.pallas import tpu as pltpu
from jax.sharding import PartitionSpec as P

B1 = 512
B2 = 1024
CH = 192


def plain_shards(inputs, cotangent, kernel, right_factor, left_factor):
    grad_scale = float(CH * B2) ** (-0.5)
    chan_dev = inputs.shape[0]
    seq_count = lax.axis_size("seq")
    loc_rows = B1 // seq_count
    loc_cols = B2 // seq_count
    flat_in = inputs.reshape(chan_dev * loc_rows, B2)
    kern_view = kernel.reshape(chan_dev, loc_rows, B2)
    whole_right = lax.all_gather(right_factor, ("seq", "ch"), axis=0, tiled=True)
    projected = jnp.dot(flat_in, whole_right, preferred_element_type=jnp.float32)
    projected = projected.reshape(chan_dev, loc_rows, B2)
    gated_mix = (projected * kern_view.astype(jnp.float32)).astype(jnp.bfloat16)
    turned = lax.all_to_all(gated_mix, "seq", split_axis=2, concat_axis=1, tiled=True)
    left_whole = lax.all_gather(left_factor, ("seq", "ch"), axis=0, tiled=True)
    mixed = jnp.einsum("pi,cij->cjp", left_whole, turned, preferred_element_type=jnp.float32)
    mixed_out = mixed.astype(jnp.bfloat16).reshape(chan_dev, loc_cols * B1)
    grad_view = cotangent.reshape(chan_dev, loc_cols, B1)
    grad_mix = jnp.einsum(
        "pi,cjp->cij", left_whole, grad_view, preferred_element_type=jnp.float32
    ).astype(jnp.bfloat16)
    left_terms = (
        jnp.einsum("cjp,cij->pi", grad_view, turned, preferred_element_type=jnp.float32)
        * grad_scale
    )
    grad_left = lax.psum_scatter(left_terms, ("seq", "ch"), scatter_dimension=0, tiled=True)
    back_grad = lax.all_to_all(grad_mix, "seq", split_axis=1, concat_axis=2, tiled=True)
    back_wide = back_grad.astype(jnp.float32)
    grad_kernel = (back_wide * projected).astype(jnp.bfloat16).reshape(chan_dev, loc_rows * B2)
    grad_proj = (
        (back_wide * kern_view.astype(jnp.float32))
        .astype(jnp.bfloat16)
        .reshape(chan_dev * loc_rows, B2)
    )
    grad_flat = lax.dot_general(
        grad_proj, whole_right, (((1,), (1,)), ((), ())), preferred_element_type=jnp.float32
    )
    grad_inputs = grad_flat.astype(jnp.bfloat16).reshape(chan_dev, loc_rows * B2)
    return (mixed_out, grad_inputs, grad_kernel, grad_left)


CHUNK = 16
LANES = 128
F32 = jnp.float32
BF16 = jnp.bfloat16
MESH = pl.DeviceIdType.MESH


def mixer_kernel(
    seqs, chs, chunks, x_hbm, g_hbm, k_hbm, right_ref, left_ref,
    mixed_hbm, gin_hbm, gker_hbm, gleft_ref,
    xbuf, kbuf, out_a, out_b, right_all, left_all, left_turned, turn_i, turn_j,
    g_rows, a_send, a_recv, d_send, d_recv, gl_turned, gl_sum, gl_ch, gl_mid, gl_side, gl_stand,
    io_sem, out_sem, wsend_sem, wrecv_sem, fsend_sem, frecv_sem,
    asend_sem, arecv_sem, dsend_sem, drecv_sem, csend_sem, crecv_sem, ssend_sem, srecv_sem,
    own_sem, part_sem,
):
    me = lax.axis_index("seq")
    mych = lax.axis_index("ch")
    rows = B1 // seqs
    cols = B2 // seqs
    grad_scale = float(CH * B2) ** (-0.5)
    wide = CHUNK * cols

    def seq_peer(t):
        return lax.rem(me + t, seqs)

    def flip(mask):
        place, bit = 0, 1
        while bit < seqs:
            digit = lax.rem(lax.div(me, bit), 2)
            place = place + bit * (1 - digit if mask & bit else digit)
            bit *= 2
        return place

    def ch_peer(t):
        return lax.rem(mych + t, chs)

    barrier = pltpu.get_barrier_semaphore()

    def hail_seq(t, _):
        pl.semaphore_signal(barrier, inc=1, device_id={"seq": seq_peer(t)}, device_id_type=MESH)
        return 0

    def hail_ch(t, _):
        pl.semaphore_signal(barrier, inc=1, device_id={"ch": ch_peer(t)}, device_id_type=MESH)
        return 0

    lax.fori_loop(1, seqs, hail_seq, 0)
    lax.fori_loop(1, chs, hail_ch, 0)

    def load(src, q, buf, n):
        return pltpu.make_async_copy(src.at[pl.ds(q * CHUNK, CHUNK), :], buf, io_sem.at[n])

    load(g_hbm, 0, xbuf, 0).start()
    left_all[me, mych] = left_ref[...]
    right_all[me, mych] = right_ref[...]
    pl.semaphore_wait(barrier, seqs + chs - 2)

    def left_seq(frm, to):
        return pltpu.make_async_remote_copy(
            left_all.at[frm, mych], left_all.at[frm, mych], wsend_sem.at[0, to],
            wrecv_sem.at[0, frm], device_id={"seq": to}, device_id_type=MESH)

    hops, held, number = [], [0], 0
    bit = seqs // 2
    while bit:
        hops.append([(number + n, mask, bit) for n, mask in enumerate(held)])
        number += len(held)
        held = held + [mask + bit for mask in held]
        bit //= 2

    def right_seq(n, block, to):
        return pltpu.make_async_remote_copy(
            right_all.at[block, mych], right_all.at[block, mych], wsend_sem.at[1, n],
            wrecv_sem.at[1, block], device_id={"seq": to}, device_id_type=MESH)

    def right_hop(h):
        for n, mask, to in hops[h]:
            right_seq(n, flip(mask), flip(to)).start()

    def right_hop_done(h):
        for n, mask, to in hops[h]:
            right_seq(n, flip(mask + to), me).wait_recv()

    def left_ch(frm, to):
        return pltpu.make_async_remote_copy(
            left_all.at[:, frm], left_all.at[:, frm], fsend_sem.at[0, to],
            frecv_sem.at[0, frm], device_id={"ch": to}, device_id_type=MESH)

    def right_ch(frm, to):
        return pltpu.make_async_remote_copy(
            right_all.at[:, frm], right_all.at[:, frm], fsend_sem.at[1, to],
            frecv_sem.at[1, frm], device_id={"ch": to}, device_id_type=MESH)

    def each_seq(f):
        def step(t, _):
            f(seq_peer(t))
            return 0
        lax.fori_loop(1, seqs, step, 0)

    def each_ch(f):
        def step(t, _):
            f(ch_peer(t))
            return 0
        lax.fori_loop(1, chs, step, 0)

    each_seq(lambda d: left_seq(me, d).start())
    right_hop(0)

    def turn_grad(q):
        load(g_hbm, q, xbuf, 0).wait()

        def spread(j, _):
            for b in range(B1 // LANES):
                turn_j[b, pl.ds(pl.multiple_of(j * CHUNK, CHUNK), CHUNK), :] = xbuf[
                    :, pl.ds(pl.multiple_of(j * B1 + b * LANES, LANES), LANES)].astype(F32)
            return 0

        lax.fori_loop(0, cols, spread, 0, unroll=4)

        def gather(c, _):
            for b in range(B1 // LANES):
                g_rows[q, pl.ds(pl.multiple_of(c * cols, cols), cols), b * LANES:(b + 1) * LANES] = turn_j[
                    b, pl.ds(c, cols, stride=CHUNK), :].astype(BF16)
            return 0

        lax.fori_loop(0, CHUNK, gather, 0)

    pieces = rows // CHUNK

    def d_copy(q, g, frm, to):
        return pltpu.make_async_remote_copy(
            d_send.at[q, pl.ds(pl.multiple_of(to * rows + g * CHUNK, CHUNK), CHUNK), :],
            d_recv.at[q, pl.ds(pl.multiple_of(frm * rows + g * CHUNK, CHUNK), CHUNK), :],
            dsend_sem.at[q, g, to], drecv_sem.at[q, g, frm],
            device_id={"seq": to}, device_id_type=MESH)

    def a_copy(q, frm, to):
        return pltpu.make_async_remote_copy(
            a_send.at[q, pl.ds(pl.multiple_of(to * rows, rows), rows), :],
            a_recv.at[q, pl.ds(pl.multiple_of(frm * rows, rows), rows), :],
            asend_sem.at[q, to], arecv_sem.at[q, frm], device_id={"seq": to}, device_id_type=MESH)

    def own_copy(send, recv, q, n):
        mine = pl.ds(pl.multiple_of(me * rows, rows), rows)
        return pltpu.make_async_copy(send.at[q, mine, :], recv.at[q, mine, :], own_sem.at[n, q])

    def make_d(q):
        def pair(h, _):
            at = pl.multiple_of(h * 2 * cols, 2 * cols)
            d_send[q, :, pl.ds(at, 2 * cols)] = lax.dot_general(
                left_turned[...], g_rows[q, pl.ds(at, 2 * cols), :],
                (((1,), (1,)), ((), ())), preferred_element_type=F32).astype(BF16)
            return 0

        lax.fori_loop(0, CHUNK // 2, pair, 0)

    def project(g):
        lhs = jnp.concatenate(
            [xbuf[:, pl.ds(pl.multiple_of((g * CHUNK + n) * B2, B2), B2)] for n in range(CHUNK)], axis=0)
        return jnp.dot(lhs, right_all[...].reshape(B2, B2), preferred_element_type=F32)

    def gates(g):
        return jnp.concatenate(
            [kbuf[:, pl.ds(pl.multiple_of((g * CHUNK + n) * B2, B2), B2)] for n in range(CHUNK)], axis=0)

    tall = CHUNK * CHUNK

    def make_a(q):
        load(x_hbm, q, xbuf, 0).wait()
        load(k_hbm, q, kbuf, 1).wait()

        def group(g, _):
            gated = project(g) * gates(g).astype(F32)
            for d in range(seqs):
                turn_i[d, pl.ds(pl.multiple_of(g * tall, tall), tall), :] = gated[:, d * cols:(d + 1) * cols]
            return 0

        lax.fori_loop(0, rows // CHUNK, group, 0)

        def gather(c, _):
            at = pl.multiple_of(c * cols, cols)
            for d in range(seqs):
                a_send[q, d * rows:(d + 1) * rows, pl.ds(at, cols)] = turn_i[
                    d, pl.ds(c, rows, stride=CHUNK), :].astype(BF16)
            return 0

        lax.fori_loop(0, CHUNK, gather, 0)

    def sent(kind, q, d):
        if kind == "a":
            a_copy(q, me, d).wait_send()
        else:
            for g in range(pieces):
                d_copy(q, g, me, d).wait_send()

    def send_a(q, earlier):
        own_copy(a_send, a_recv, q, 0).start()

        def one(d):
            if earlier is not None:
                sent(*earlier, d)
            a_copy(q, me, d).start()

        each_seq(one)

    def send_d(q, earlier):
        own_copy(d_send, d_recv, q, 1).start()

        def first(d):
            if earlier is not None:
                sent(*earlier, d)
            d_copy(q, 0, me, d).start()

        each_seq(first)

        def later(g, _):
            each_seq(lambda d: d_copy(q, g, me, d).start())
            return 0

        lax.fori_loop(1, pieces, later, 0)

    def store(buf, dst, q, n):
        return pltpu.make_async_copy(buf, dst.at[pl.ds(q * CHUNK, CHUNK), :], out_sem.at[n])

    def finish_a(q):
        own_copy(a_send, a_recv, q, 0).wait()
        each_seq(lambda d: a_copy(q, d, me).wait_recv())

        def pair(h, _):
            at = pl.multiple_of(h * 2 * cols, 2 * cols)
            block = a_recv[q, :, pl.ds(at, 2 * cols)]
            got = jnp.dot(left_all[...].reshape(B1, B1), block, preferred_element_type=F32).T
            for b in range(B1 // LANES):
                lanes = slice(b * LANES, (b + 1) * LANES)
                turn_j[b, pl.ds(2 * h, cols, stride=CHUNK), :] = got[:cols, lanes]
                turn_j[b, pl.ds(2 * h + 1, cols, stride=CHUNK), :] = got[cols:, lanes]
            gl_turned[...] += jnp.dot(
                block, g_rows[q, pl.ds(at, 2 * cols), :], preferred_element_type=F32)
            return 0

        lax.fori_loop(0, CHUNK // 2, pair, 0)

        def spread(j, _):
            for b in range(B1 // LANES):
                out_a[:, pl.ds(pl.multiple_of(j * B1 + b * LANES, LANES), LANES)] = turn_j[
                    b, pl.ds(pl.multiple_of(j * CHUNK, CHUNK), CHUNK), :].astype(BF16)
            return 0

        lax.fori_loop(0, cols, spread, 0, unroll=4)
        store(out_a, mixed_hbm, q, 0).start()
        store(out_a, mixed_hbm, q, 0).wait()

    def finish_d(q):
        load(x_hbm, q, xbuf, 0).start()
        load(k_hbm, q, kbuf, 1).start()
        load(x_hbm, q, xbuf, 0).wait()
        load(k_hbm, q, kbuf, 1).wait()
        own_copy(d_send, d_recv, q, 1).wait()

        def part(buf, dst, g, n):
            span = pl.ds(pl.multiple_of(g * CHUNK * B2, CHUNK * B2), CHUNK * B2)
            return pltpu.make_async_copy(
                buf.at[:, span], dst.at[pl.ds(q * CHUNK, CHUNK), span], part_sem.at[n, g])

        def group(g, _):
            each_seq(lambda d: d_copy(q, g, d, me).wait_recv())
            at = pl.multiple_of(g * tall, tall)

            def gather(c, _):
                lanes = pl.ds(pl.multiple_of(c * cols, cols), cols)
                for s in range(seqs):
                    turn_i[s, pl.ds(at + c, CHUNK, stride=CHUNK), :] = d_recv[
                        q, pl.ds(pl.multiple_of(s * rows + g * CHUNK, CHUNK), CHUNK), lanes].astype(F32)
                return 0

            lax.fori_loop(0, CHUNK, gather, 0, unroll=4)
            back = jnp.concatenate([turn_i[s, pl.ds(at, tall), :] for s in range(seqs)], axis=1)
            inner = (back * gates(g).astype(F32)).astype(BF16)
            second = lax.dot_general(
                inner, right_all[...].reshape(B2, B2), (((1,), (1,)), ((), ())),
                preferred_element_type=F32).astype(BF16)
            for n in range(CHUNK):
                out_b[:, pl.ds(pl.multiple_of((g * CHUNK + n) * B2, B2), B2)] = second[
                    n * CHUNK:(n + 1) * CHUNK]
            part(out_b, gin_hbm, g, 1).start()
            first = (back * project(g)).astype(BF16)
            for n in range(CHUNK):
                out_a[:, pl.ds(pl.multiple_of((g * CHUNK + n) * B2, B2), B2)] = first[
                    n * CHUNK:(n + 1) * CHUNK]
            part(out_a, gker_hbm, g, 0).start()
            return 0

        lax.fori_loop(0, pieces, group, 0)

        def written(g, _):
            part(out_a, gker_hbm, g, 0).wait()
            part(out_b, gin_hbm, g, 1).wait()
            return 0

        lax.fori_loop(0, pieces, written, 0)

    def load_a(q):
        load(x_hbm, q, xbuf, 0).start()
        load(k_hbm, q, kbuf, 1).start()

    turn_grad(0)
    load_a(0)
    each_seq(lambda d: left_seq(d, me).wait_recv())
    each_ch(lambda c: left_ch(mych, c).start())
    for h in range(1, len(hops) - 1):
        right_hop_done(h - 1)
        right_hop(h)
    each_ch(lambda c: left_ch(c, mych).wait_recv())
    left_turned[...] = left_all[...].reshape(B1, B1).astype(F32).T.astype(BF16)
    right_hop_done(len(hops) - 2)
    right_hop(len(hops) - 1)
    make_d(0)
    send_d(0, None)
    right_hop_done(len(hops) - 1)
    each_ch(lambda c: right_ch(mych, c).start())
    each_ch(lambda c: right_ch(c, mych).wait_recv())
    gl_turned[...] = jnp.zeros_like(gl_turned)

    order = [("d", 0)] + [("a", q) for q in range(chunks)] + [("d", q) for q in range(1, chunks)]
    make_a(0)
    send_a(0, None)
    ready = {("a", 0), ("d", 0)}

    def prepare(kind, q):
        if (kind, q) in ready:
            return
        ready.add((kind, q))
        if kind == "a":
            load_a(q)
            make_a(q)
        else:
            load(g_hbm, q, xbuf, 0).start()
            turn_grad(q)
            make_d(q)

    def finish(kind, q):
        if kind == "a":
            finish_a(q)
        else:
            finish_d(q)

    for n, (kind, q) in enumerate(order):
        if n >= 2:
            prepare(kind, q)
            (send_a if kind == "a" else send_d)(q, order[n - 2])
            if n + 1 < len(order):
                prepare(*order[n + 1])
            finish(*order[n - 2])

    def gl_to_ch(frm, to):
        return pltpu.make_async_remote_copy(
            gl_sum.at[:, to], gl_ch.at[frm], csend_sem.at[to], crecv_sem.at[frm],
            device_id={"ch": to}, device_id_type=MESH)

    side = lax.rem(me, 2)
    stand = lax.div(me, 2)

    def gl_to_side(frm, to):
        return pltpu.make_async_remote_copy(
            gl_mid.at[:, to], gl_side, ssend_sem.at[seqs - 1], srecv_sem.at[seqs - 1],
            device_id={"seq": flip(1)}, device_id_type=MESH)

    def gl_to_stand(frm, to):
        return pltpu.make_async_remote_copy(
            gl_side.at[to], gl_stand.at[frm], ssend_sem.at[to], srecv_sem.at[frm],
            device_id={"seq": to * 2 + side}, device_id_type=MESH)

    def each_stand(f):
        def step(t, _):
            f(lax.rem(stand + t, seqs // 2))
            return 0
        lax.fori_loop(1, seqs // 2, step, 0)

    gl_sum[...] = (gl_turned[...].T * grad_scale).reshape(gl_sum.shape)
    each_ch(lambda c: gl_to_ch(mych, c).start())
    gl_ch[mych] = gl_sum[:, mych]
    each_ch(lambda c: gl_to_ch(c, mych).wait_recv())
    total = gl_ch[0]
    for c in range(1, chs):
        total = total + gl_ch[c]
    gl_mid[...] = total.reshape(gl_mid.shape)
    gl_to_side(side, 1 - side).start()
    gl_to_side(1 - side, side).wait_recv()
    gl_side[...] += gl_mid[:, side]
    each_stand(lambda z: gl_to_stand(stand, z).start())
    gl_stand[stand] = gl_side[stand]

    finish(*order[-2])
    each_stand(lambda z: gl_to_stand(z, stand).wait_recv())
    whole = gl_stand[0]
    for z in range(1, seqs // 2):
        whole = whole + gl_stand[z]
    gleft_ref[...] = whole
    finish(*order[-1])

    for kind, q in order[-2:]:
        each_seq(lambda d: sent(kind, q, d))
    each_seq(lambda d: left_seq(me, d).wait_send())
    for hop in hops:
        for n, mask, to in hop:
            right_seq(n, flip(mask), flip(to)).wait_send()
    each_ch(lambda c: left_ch(mych, c).wait_send())
    each_ch(lambda c: right_ch(mych, c).wait_send())
    each_ch(lambda c: gl_to_ch(mych, c).wait_send())
    gl_to_side(side, 1 - side).wait_send()
    each_stand(lambda z: gl_to_stand(stand, z).wait_send())


def shards(inputs, cotangent, kernel, right_factor, left_factor):
    seqs, chs = lax.axis_size("seq"), lax.axis_size("ch")
    chan_dev, span = inputs.shape
    rows, cols = B1 // seqs, B2 // seqs
    if chan_dev % CHUNK or cols != LANES or seqs & (seqs - 1) or seqs < 4 or rows % CHUNK or chan_dev < 3 * CHUNK:
        return plain_shards(inputs, cotangent, kernel, right_factor, left_factor)
    chunks = chan_dev // CHUNK
    wide = CHUNK * cols
    any_spec = pl.BlockSpec(memory_space=pl.ANY)
    vmem_spec = pl.BlockSpec(memory_space=pltpu.VMEM)
    dma = pltpu.SemaphoreType.DMA
    big = jax.ShapeDtypeStruct((chan_dev, span), BF16)
    part = B1 // (seqs * chs)
    flops = 2 * chan_dev * B1 * B2 * (3 * B2 + 3 * B1) // seqs
    return pl.pallas_call(
        functools.partial(mixer_kernel, seqs, chs, chunks),
        out_shape=(big, big, big, jax.ShapeDtypeStruct((part, B1), F32)),
        in_specs=[any_spec] * 3 + [vmem_spec] * 2,
        out_specs=(any_spec, any_spec, any_spec, vmem_spec),
        scratch_shapes=[
            pltpu.VMEM((CHUNK, span), BF16),
            pltpu.VMEM((CHUNK, span), BF16),
            pltpu.VMEM((CHUNK, span), BF16),
            pltpu.VMEM((CHUNK, span), BF16),
            pltpu.VMEM((seqs, chs, B2 // (seqs * chs), B2), BF16),
            pltpu.VMEM((seqs, chs, part, B1), BF16),
            pltpu.VMEM((B1, B1), BF16),
            pltpu.VMEM((seqs, CHUNK * rows, cols), F32),
            pltpu.VMEM((B1 // LANES, CHUNK * cols, LANES), F32),
            pltpu.VMEM((chunks, wide, B1), BF16),
            pltpu.VMEM((chunks, B1, wide), BF16),
            pltpu.VMEM((chunks, B1, wide), BF16),
            pltpu.VMEM((chunks, B1, wide), BF16),
            pltpu.VMEM((chunks, B1, wide), BF16),
            pltpu.VMEM((B1, B1), F32),
            pltpu.VMEM((seqs, chs, part, B1), F32),
            pltpu.VMEM((chs, seqs, part, B1), F32),
            pltpu.VMEM((seqs // 2, 2, part, B1), F32),
            pltpu.VMEM((seqs // 2, part, B1), F32),
            pltpu.VMEM((seqs // 2, part, B1), F32),
            dma((2,)), dma((1,)),
            dma((2, seqs)), dma((2, seqs)), dma((2, chs)), dma((2, chs)),
            dma((chunks, seqs)), dma((chunks, seqs)),
            dma((chunks, rows // CHUNK, seqs)), dma((chunks, rows // CHUNK, seqs)),
            dma((chs,)), dma((chs,)), dma((seqs,)), dma((seqs,)),
            dma((2, chunks)), dma((2, rows // CHUNK)),
        ],
        compiler_params=pltpu.CompilerParams(
            collective_id=0, has_side_effects=True, vmem_limit_bytes=62 * 1024 * 1024),
        cost_estimate=pl.CostEstimate(flops=flops, bytes_accessed=12 * chan_dev * span, transcendentals=0),
        name="monarch_mixer",
    )(inputs, cotangent, kernel, right_factor, left_factor)


def solution(mesh):
    placed = (
        P("ch", ("grp", "seq")),
        P("ch", ("grp", "seq")),
        P("ch", "seq"),
        P(("seq", "ch"), None),
        P(("seq", "ch"), None),
    )
    return jax.shard_map(
        shards,
        mesh=mesh,
        in_specs=placed,
        out_specs=(
            P("ch", ("grp", "seq")),
            P("ch", ("grp", "seq")),
            P("ch", ("grp", "seq")),
            P(("grp", "seq", "ch"), None),
        ),
        check_vma=False,
    )
```
